256 devices in a mesh: blk: 32 (over z_hi, y, x), tm: 8 (over z_lo, core).
Axes of the slice: x: 4, y: 4, z: 8 (z_hi: 2, z_lo: 4; z = z_hi * 4 + z_lo), core: 2. Of those that a mesh axis runs over, the one named last changes fastest.
Arguments:
- returns: bfloat16 [16384, 2048], P('blk', 'tm'), may hold values from -6 to 6
- plan: int32 [2, 32], replicated, may hold values from 0 to 31, as said below
- pair_mask: int32 [32, 32], replicated, may hold values 0 or 1
Outputs:
- lead_lag: bfloat16 [16384, 2, 7680], P(('blk', 'tm'))
The draws below stay inside these ranges and needn't reach their ends.
Inputs may be any that keep to these rules, and one draw needn't show every extreme that they name: Each round r has a word m_r with plan[r, b] = b XOR m_r for every block b; m_r is never 0, and every bit of a block index is set in the word of some round.
All inputs are finite; a program needn't handle non-finite values.
Results may differ from the reference program's by a relative error of at most 0.001.
Values may be sent and summed in bfloat16 or wider, within the bound.
No kernel may reach another device: no remote copies, remote signals or barrier semaphores. Data moves between devices by JAX's collectives and lax.ppermute only.
A program may use at most 64 MiB of HBM per device.

```python
import jax
import jax.numpy as jnp
from jax import lax

BLK = 512
LAG = 7
LAGS = 15
ROUNDS = 2
NBLOCKS = 32
NI = 16384
NT = 2048


def draw_plan(key, part):
    first = jax.random.randint(key, (), 1, NBLOCKS - 1)
    rounds_idx = jnp.arange(ROUNDS)
    words = jnp.where(rounds_idx % 2 == 0, first, jnp.bitwise_xor(first, NBLOCKS - 1))
    indices = jnp.arange(NBLOCKS)
    return jnp.bitwise_xor(indices[None, :], words[:, None]).astype(jnp.int32)


def with_ends(values, rng, smallest, largest):
    shape = values.shape
    index_at = [jax.random.randint(jax.random.fold_in(rng, axis), (), 0, shape[axis]) for axis in range(len(shape))]
    values = values.at[tuple(index_at)].set(smallest)
    longest = shape.index(max(shape))
    index_at[longest] = (index_at[longest] + 1) % shape[longest]
    return values.at[tuple(index_at)].set(largest)


def steps_of(stream_key, shape, pieces, low, top_value):
    gain = 1.0
    for position, shards_of in pieces:
        steps = jax.random.uniform(jax.random.fold_in(jax.random.fold_in(stream_key, 6), position), (shards_of,), jnp.float32, low / len(pieces), top_value / len(pieces))
        gain = gain * jnp.repeat(jnp.exp(steps), shape[position] // shards_of).reshape((-1,) + (1,) * (len(shape) - 1 - position))
    return gain


def noise(rng, extent, width, reach, split=(), kind=jnp.bfloat16):
    level = steps_of(rng, extent, split, -0.22, 0.18) if split else 1.0
    entries = jax.random.normal(rng, extent, jnp.float32) * width * level
    return jnp.minimum(jnp.maximum(entries, -reach), reach).astype(kind)


def setup_inputs(seed: int = 0) -> dict:
    keys = jax.random.split(jax.random.key(seed), 4)
    return {
        "returns": noise(keys[0], (NI, NT), 1.0, 6.0, ((0, 32), (1, 8))),
        "plan": draw_plan(jax.random.fold_in(keys[3], 71), 0),
        "pair_mask": with_ends((jax.random.randint(keys[2], (NBLOCKS, NBLOCKS), 0, 4) < 3).astype(jnp.int32), jax.random.fold_in(keys[2], 1), 0, 1),
    }


def block_gram(returns, partner_of, live_of, block_idx):
    partner = partner_of[block_idx]
    own_rows = lax.dynamic_slice(returns, (block_idx * BLK, jnp.int32(0)), (BLK, NT))
    mate_rows = lax.dynamic_slice(returns, (partner * BLK, jnp.int32(0)), (BLK, NT))
    padded = jnp.pad(mate_rows, ((0, 0), (LAG, LAG)))
    stacked = jnp.concatenate([padded[:, offset:offset + NT] for offset in range(2 * LAG + 1)], axis=0)
    gram = lax.dot_general(own_rows, stacked, (((1,), (1,)), ((), ())), preferred_element_type=jnp.float32)
    weight = live_of[block_idx].astype(jnp.float32) * (float(NT) ** -0.5)
    return (gram * weight).astype(jnp.bfloat16)


def reference(returns, plan, pair_mask):
    collected = []
    indices = jnp.arange(NBLOCKS, dtype=jnp.int32)
    for round_id in range(ROUNDS):
        partner_of = plan[round_id].astype(jnp.int32)
        live_of = pair_mask[indices, partner_of]
        grams = lax.map(lambda block_idx: block_gram(returns, partner_of, live_of, block_idx), indices)
        collected.append(grams.reshape(NI, LAGS * BLK))
    return jnp.stack(collected, axis=1)
```

```python
import functools

import jax
import jax.numpy as jnp
from jax import lax
from jax.experimental import pallas as pl
from jax.experimental.pallas import tpu as pltpu
from jax.sharding import Mesh
from jax.sharding import PartitionSpec as P

LAG = 7
LAGS = 2 * LAG + 1
TM = ("tm_0", "tm_1")
BLK_TM = ("blk", "tm_0", "tm_1")
GROUP = 3

FIRST_TO = (1, 3, 0, 2)
SECOND_TO = (3, 1, 2, 0)
FIRST_FROM = (2, 0, 3, 1)
SECOND_FROM = (3, 1, 2, 0)


def swapped(value, axis, word):
    count = lax.axis_size(axis)
    return lax.ppermute(value, axis, [(i, i ^ word) for i in range(count)])


def crossed(value, target):
    route = []
    for block in range(lax.axis_size("blk")):
        for z in range(4):
            route.append((block * 4 + z, (block ^ 16) * 4 + target[z]))
    return lax.ppermute(value, ("blk", "tm_0"), route)


def by_word(value, word, count):
    branches = [lambda v: v] + [functools.partial(swapped, axis="blk", word=k) for k in range(1, count)]
    return lax.switch(word, branches, value)


def own_rows(returns, z, core):
    pieces = returns.reshape(4, 2, 64, returns.shape[1])
    got = [lax.dynamic_index_in_dim(pieces, z, 0, keepdims=False)]
    for k in range(1, 4):
        send = lax.dynamic_index_in_dim(pieces, z ^ k, 0, keepdims=False)
        got.append(swapped(send, "tm_0", k))
    chip = jnp.stack(got, axis=0)
    mine = lax.dynamic_index_in_dim(chip, core, 1, keepdims=False)
    other = swapped(lax.dynamic_index_in_dim(chip, 1 - core, 1, keepdims=False), "tm_1", 1)
    both = jnp.stack([mine, other], axis=1)
    both = jnp.where(core == 1, both[:, ::-1], both)
    both = both.reshape(2, 2, *both.shape[1:])
    both = jnp.where(z & 1 == 1, both[:, ::-1], both)
    both = jnp.where(z & 2 == 2, both[::-1], both)
    both = both.reshape(8, *both.shape[3:])
    return jnp.moveaxis(both, 0, 1).reshape(both.shape[1], -1)


def sums(order_ref, own_ref, slab_refs):
    total = None
    for k, slab in enumerate(slab_refs):
        start = pl.multiple_of(order_ref[k] * 256, 256)
        left = own_ref[:, :, pl.ds(start, 256)].reshape(GROUP * 64, 256)
        part = lax.dot_general(left, slab[...], (((1,), (1,)), ((), ())), preferred_element_type=jnp.float32)
        total = part if total is None else total + part
    return total


def part_kernel(count, order_ref, own_ref, *refs):
    out_ref = refs[count]
    out_ref[...] = sums(order_ref, own_ref, refs[:count])


def last_kernel(count, order_ref, weight_ref, own_ref, done_ref, part_ref, *refs):
    out_ref = refs[count]
    late = (sums(order_ref, own_ref, refs[:count]) + part_ref[...]) * weight_ref[1]
    early = done_ref[...] * weight_ref[0]
    swap = order_ref[count] == 1
    first = jnp.where(swap, late, early)
    second = jnp.where(swap, early, late)
    for k in range(GROUP):
        rows = slice(k * 64, k * 64 + 64)
        both = jnp.stack([first[rows], second[rows]], axis=1)
        out_ref[:, :, k * 512 : k * 512 + 512] = both.astype(out_ref.dtype)


def own_spec(own):
    return pl.BlockSpec((GROUP, own.shape[1], own.shape[2]), lambda g, *_: (g, 0, 0))


def part_spec():
    return pl.BlockSpec((GROUP * 64, 512), lambda g, *_: (g, 0))


def slab_spec():
    return pl.BlockSpec((512, 256), lambda g, *_: (0, 0))


def params():
    return pltpu.CompilerParams(vmem_limit_bytes=48 * 1024 * 1024)


def cost(count):
    return pl.CostEstimate(flops=2 * 960 * 512 * 256 * count, bytes_accessed=6_000_000, transcendentals=0)


def part_sums(order, own, slabs):
    count = len(slabs)
    return pl.pallas_call(
        functools.partial(part_kernel, count),
        grid_spec=pltpu.PrefetchScalarGridSpec(
            num_scalar_prefetch=1,
            grid=(LAGS // GROUP,),
            in_specs=[own_spec(own)] + [slab_spec()] * count,
            out_specs=part_spec(),
        ),
        out_shape=jax.ShapeDtypeStruct((LAGS * 64, 512), jnp.float32),
        compiler_params=params(),
        cost_estimate=cost(count),
    )(order, own, *slabs)


def last_sums(order, weights, own, done, part, slabs):
    count = len(slabs)
    return pl.pallas_call(
        functools.partial(last_kernel, count),
        grid_spec=pltpu.PrefetchScalarGridSpec(
            num_scalar_prefetch=2,
            grid=(LAGS // GROUP,),
            in_specs=[own_spec(own), part_spec(), part_spec()] + [slab_spec()] * count,
            out_specs=pl.BlockSpec((64, 2, GROUP * 512), lambda g, *_: (0, 0, g)),
        ),
        out_shape=jax.ShapeDtypeStruct((64, 2, LAGS * 512), jnp.bfloat16),
        compiler_params=params(),
        cost_estimate=cost(count),
    )(order, weights, own, done, part, *slabs)


def on_device(returns, plan, pair_mask):
    block = lax.axis_index("blk")
    z = lax.axis_index("tm_0")
    core = lax.axis_index("tm_1")
    minutes_all = returns.shape[1] * 8
    factor = float(minutes_all) ** (-0.5)

    words = (plan[0, 0], plan[1, 0])
    swap = (words[1] & 16) == 0
    near_word = jnp.where(swap, words[1], words[0])
    far_word = jnp.where(swap, words[0], words[1])
    near_live = pair_mask[block, block ^ near_word].astype(jnp.float32)
    far_live = pair_mask[block, block ^ far_word].astype(jnp.float32)
    weights = jnp.stack([near_live, far_live]) * factor

    own = own_rows(returns, z, core)
    padded = jnp.pad(own, ((0, 0), (LAG, LAG)))
    shifted = jnp.stack(
        [lax.slice_in_dim(padded, 2 * LAG - k, 2 * LAG - k + minutes_all, axis=1) for k in range(LAGS)], axis=0
    )

    far = by_word(returns, far_word & 15, 16)
    far_1 = crossed(far, FIRST_TO)
    far_2 = crossed(far, SECOND_TO)
    near = by_word(returns, near_word, 32)
    near_all = [near] + [swapped(near, "tm_0", k) for k in range(1, 4)]
    far_3 = swapped(far_1, "tm_0", 1)
    far_4 = swapped(far_2, "tm_0", 1)

    def pick(table, at):
        return jnp.asarray(table, jnp.int32)[at]

    def both_cores(slabs):
        return list(slabs) + [swapped(s, "tm_1", 1) for s in slabs]

    def order_of(places, extra=()):
        here = [2 * p + core for p in places]
        there = [2 * p + (1 - core) for p in places]
        return jnp.stack([jnp.int32(v) for v in here + there + list(extra)])

    near_done = part_sums(order_of([z ^ k for k in range(4)]), shifted, both_cores(near_all))
    far_part = part_sums(
        order_of([pick(FIRST_FROM, z), pick(SECOND_FROM, z)]), shifted, both_cores([far_1, far_2])
    )
    return last_sums(
        order_of([pick(FIRST_FROM, z ^ 1), pick(SECOND_FROM, z ^ 1)], [swap.astype(jnp.int32)]),
        weights,
        shifted,
        near_done,
        far_part,
        both_cores([far_3, far_4]),
    )


def solution(mesh):
    split = Mesh(mesh.devices.reshape(mesh.shape["blk"], 4, 2), ("blk", "tm_0", "tm_1"))
    return jax.shard_map(
        on_device,
        mesh=split,
        in_specs=(P("blk", TM), P(), P()),
        out_specs=P(BLK_TM, None, None),
        check_vma=False,
    )
```

```python
import functools

import jax
import jax.numpy as jnp
from jax import lax
from jax.experimental import pallas as pl
from jax.experimental.pallas import tpu as pltpu
from jax.sharding import Mesh
from jax.sharding import PartitionSpec as P

LAG = 7
LAGS = 2 * LAG + 1
TM = ("tm_0", "tm_1")
BLK_TM = ("blk", "tm_0", "tm_1")
GROUP = 3
VMEM_BYTES = 20 * 1024 * 1024

def swapped(value, axis, word):
    count = lax.axis_size(axis)
    return lax.ppermute(value, axis, [(i, i ^ word) for i in range(count)])


def crossed(value, word):
    count = lax.axis_size("blk") * 4
    return lax.ppermute(value, ("blk", "tm_0"), [(i, i ^ 64 ^ word) for i in range(count)])


def together(*values):
    return lax.optimization_barrier(values)


def by_word(value, word, count, move):
    return lax.switch(word, [functools.partial(move, word=k) for k in range(count)], value)


def to_near(value, word):
    return swapped(value, "blk", word) if word else value


def vmem():
    return pl.BlockSpec(memory_space=pltpu.VMEM)


def smem():
    return pl.BlockSpec(memory_space=pltpu.SMEM)


def params():
    return pltpu.CompilerParams(vmem_limit_bytes=VMEM_BYTES)


def cost(flops, size):
    return pl.CostEstimate(flops=flops, bytes_accessed=size, transcendentals=0)


def own_kernel(place_ref, here_ref, there_ref, out_ref, row_ref):
    z, core = place_ref[0], place_ref[1]
    rows, edge = row_ref.shape[0], 128
    row_ref[:, :edge] = jnp.zeros((rows, edge), row_ref.dtype)
    row_ref[:, edge + 2048 :] = jnp.zeros((rows, edge), row_ref.dtype)
    mine = pl.ds(pl.multiple_of(512 + core * rows, 64), rows)
    for k in range(4):
        slab = 2 * (z ^ k)
        for pack, at in ((here_ref, slab + core), (there_ref, slab + 1 - core)):
            row_ref[:, pl.ds(pl.multiple_of(edge + at * 256, 128), 256)] = pack[k, mine, :]
    for lag in range(LAGS):
        start = edge + LAG - lag
        out_ref[lag * rows : lag * rows + rows, :] = row_ref[:, start : start + 2048]


def own_shifts(place, here, there):
    return pl.pallas_call(
        own_kernel,
        in_specs=[smem()] + [vmem()] * 2,
        out_specs=vmem(),
        out_shape=jax.ShapeDtypeStruct((LAGS * 64, 2048), jnp.bfloat16),
        scratch_shapes=[pltpu.VMEM((64, 2048 + 256), jnp.bfloat16)],
        compiler_params=params(),
        cost_estimate=cost(0, 8_000_000),
    )(place, here, there)


def products(order_ref, own_ref, slab_refs):
    total = None
    for k, slab in enumerate(slab_refs):
        start = pl.multiple_of(order_ref[k] * 256, 256)
        part = lax.dot_general(
            own_ref[:, pl.ds(start, 256)], slab[:512, :], (((1,), (1,)), ((), ())), preferred_element_type=jnp.float32
        )
        total = part if total is None else total + part
    return total


def sums_kernel(count, order_ref, own_ref, *refs):
    total = products(order_ref, own_ref, refs[:count])
    refs[-1][...] = total + refs[count][...] if len(refs) > count + 1 else total


def sums(order, own, slabs, before=()):
    count = len(slabs)
    return pl.pallas_call(
        functools.partial(sums_kernel, count),
        in_specs=[smem(), vmem()] + [vmem()] * (count + len(before)),
        out_specs=vmem(),
        out_shape=jax.ShapeDtypeStruct((LAGS * 64, 512), jnp.float32),
        compiler_params=params(),
        cost_estimate=cost(2 * 960 * 512 * 256 * count, 2_000_000),
    )(order, own, *slabs, *before)


def place_round(out_ref, index, values, lags):
    for k in range(lags):
        rows = values[k * 64 : k * 64 + 64].astype(out_ref.dtype)
        out_ref[:, index, k * 512 : k * 512 + 512] = rows


def near_kernel(order_ref, weight_ref, own_ref, here_ref, there_ref, out_ref, sum_ref):
    slabs = [ref.at[k] for ref in (here_ref, there_ref) for k in range(4)]
    sum_ref[...] = products(order_ref, own_ref, slabs) * weight_ref[0]
    for index in range(2):
        @pl.when(order_ref[8] == index)
        def _():
            place_round(out_ref, index, sum_ref, LAGS)


def near_round(order, weights, own, here, there):
    return pl.pallas_call(
        near_kernel,
        in_specs=[smem(), smem()] + [vmem()] * 3,
        out_specs=vmem(),
        out_shape=jax.ShapeDtypeStruct((64, 2, LAGS * 512), jnp.bfloat16),
        scratch_shapes=[pltpu.VMEM((LAGS * 64, 512), jnp.float32)],
        compiler_params=params(),
        cost_estimate=cost(2 * 960 * 512 * 256 * 8, 4_000_000),
    )(order, weights, own, here, there)


def last_kernel(count, order_ref, weight_ref, own_ref, near_ref, part_ref, *refs):
    out_ref, sum_ref = refs[count], refs[count + 1]
    step = pl.program_id(0)

    @pl.when(step == 0)
    def _():
        sum_ref[...] = (products(order_ref, own_ref, refs[:count]) + part_ref[...]) * weight_ref[1]

    width = GROUP * 512
    out_ref[...] = near_ref[:, :, pl.ds(pl.multiple_of(step * width, width), width)]
    rows = sum_ref.at[pl.ds(pl.multiple_of(step * GROUP * 64, GROUP * 64), GROUP * 64)]
    for index in range(2):
        @pl.when(order_ref[count] != index)
        def _():
            place_round(out_ref, index, rows, GROUP)


def last_round(order, weights, own, near, part, slabs):
    count = len(slabs)
    return pl.pallas_call(
        functools.partial(last_kernel, count),
        grid=(LAGS // GROUP,),
        in_specs=[smem(), smem()] + [vmem()] * (3 + count),
        out_specs=pl.BlockSpec((64, 2, GROUP * 512), lambda g: (0, 0, g)),
        out_shape=jax.ShapeDtypeStruct((64, 2, LAGS * 512), jnp.bfloat16),
        scratch_shapes=[pltpu.VMEM((LAGS * 64, 512), jnp.float32)],
        compiler_params=params(),
        cost_estimate=cost(2 * 960 * 512 * 256 * count, 6_000_000),
    )(order, weights, own, near, part, *slabs)


def on_device(returns, plan, pair_mask):
    block = lax.axis_index("blk")
    z = lax.axis_index("tm_0")
    core = lax.axis_index("tm_1")
    minutes_all = returns.shape[1] * 8
    factor = float(minutes_all) ** (-0.5)

    words = (plan[0, 0], plan[1, 0])
    swap = (words[1] & 16) == 0
    near_word = jnp.where(swap, words[1], words[0])
    far_word = jnp.where(swap, words[0], words[1])
    near_live = pair_mask[block, block ^ near_word].astype(jnp.float32)
    far_live = pair_mask[block, block ^ far_word].astype(jnp.float32)
    weights = jnp.stack([near_live, far_live]) * factor

    def other_core(slabs):
        return [swapped(s, "tm_1", 1) for s in slabs]

    def order_of(words, extra=()):
        here = [2 * (z ^ k) + core for k in words]
        there = [2 * (z ^ k) + (1 - core) for k in words]
        return jnp.stack([jnp.int32(v) for v in here + there + list(extra)])

    near = by_word(returns, near_word & 15, 16, to_near)
    near = lax.cond(near_word >= 16, lambda v: swapped(v, "blk", 16), lambda v: v, near)
    rows = returns.reshape(4, 128, returns.shape[1])
    packs = []
    for k in range(4):
        pack = jnp.concatenate([near, lax.dynamic_index_in_dim(rows, z ^ k, 0, keepdims=False)], axis=0)
        packs.append(swapped(pack, "tm_0", k) if k else pack)
    far_word, _ = together(far_word, near)
    far = by_word(returns, far_word & 15, 16, to_near)
    far_2, far_1 = crossed(far, 2), crossed(far, 1)
    far_3, far_0 = swapped(far_2, "tm_0", 1), swapped(far_1, "tm_0", 1)
    packs = list(together(*packs, far_2, far_1)[:4])
    near_here = jnp.stack(packs)
    near_there = swapped(near_here, "tm_1", 1)
    own = own_shifts(jnp.stack([z, core]).astype(jnp.int32), near_here, near_there)
    near_index = swap.astype(jnp.int32)
    done = near_round(order_of(range(4), [near_index]), weights, own, near_here, near_there)
    part = sums(order_of([2, 1]), own, [far_2, far_1] + other_core([far_2, far_1]))
    far_3, far_0, done, part = together(far_3, far_0, done, part)
    order = order_of([3, 0])
    part = sums(order[:2], own, [far_3, far_0], (part,))
    order = jnp.concatenate([order[2:], near_index.reshape(1)])
    return last_round(order, weights, own, done, part, other_core([far_3, far_0]))


def solution(mesh):
    split = Mesh(mesh.devices.reshape(mesh.shape["blk"], 4, 2), ("blk", "tm_0", "tm_1"))
    return jax.shard_map(
        on_device,
        mesh=split,
        in_specs=(P("blk", TM), P(), P()),
        out_specs=P(BLK_TM, None, None),
        check_vma=False,
    )
```

```python
import functools

import jax
import jax.numpy as jnp
from jax import lax
from jax.experimental import pallas as pl
from jax.experimental.pallas import tpu as pltpu
from jax.sharding import Mesh
from jax.sharding import PartitionSpec as P

LAG = 7
LAGS = 2 * LAG + 1
TM = ("tm_0", "tm_1")
BLK_TM = ("blk", "tm_0", "tm_1")
GROUP = 5
VMEM_BYTES = 20 * 1024 * 1024

def swapped(value, axis, word):
    count = lax.axis_size(axis)
    return lax.ppermute(value, axis, [(i, i ^ word) for i in range(count)])


def crossed(value, word):
    count = lax.axis_size("blk") * 4
    return lax.ppermute(value, ("blk", "tm_0"), [(i, i ^ 64 ^ word) for i in range(count)])


def together(*values):
    return lax.optimization_barrier(values)


def by_word(value, word, count, move):
    return lax.switch(word, [functools.partial(move, word=k) for k in range(count)], value)


def to_near(value, word):
    return swapped(value, "blk", word) if word else value


def vmem():
    return pl.BlockSpec(memory_space=pltpu.VMEM)


def smem():
    return pl.BlockSpec(memory_space=pltpu.SMEM)


def params():
    return pltpu.CompilerParams(vmem_limit_bytes=VMEM_BYTES)


def cost(flops, size):
    return pl.CostEstimate(flops=flops, bytes_accessed=size, transcendentals=0)


def own_kernel(place_ref, here_ref, there_ref, out_ref, row_ref):
    z, core = place_ref[0], place_ref[1]
    rows, edge = row_ref.shape[0], 128
    row_ref[:, :edge] = jnp.zeros((rows, edge), row_ref.dtype)
    row_ref[:, edge + 2048 :] = jnp.zeros((rows, edge), row_ref.dtype)
    mine = pl.ds(pl.multiple_of(512 + core * rows, 64), rows)
    for k in range(4):
        slab = 2 * (z ^ k)
        for pack, at in ((here_ref, slab + core), (there_ref, slab + 1 - core)):
            row_ref[:, pl.ds(pl.multiple_of(edge + at * 256, 128), 256)] = pack[k, mine, :]
    for lag in range(LAGS):
        start = edge + LAG - lag
        out_ref[lag * rows : lag * rows + rows, :] = row_ref[:, start : start + 2048]


def own_shifts(place, here, there):
    return pl.pallas_call(
        own_kernel,
        in_specs=[smem()] + [vmem()] * 2,
        out_specs=vmem(),
        out_shape=jax.ShapeDtypeStruct((LAGS * 64, 2048), jnp.bfloat16),
        scratch_shapes=[pltpu.VMEM((64, 2048 + 256), jnp.bfloat16)],
        compiler_params=params(),
        cost_estimate=cost(0, 8_000_000),
    )(place, here, there)


def products(order_ref, own_ref, slab_refs):
    total = None
    for k, slab in enumerate(slab_refs):
        start = pl.multiple_of(order_ref[k] * 256, 256)
        part = lax.dot_general(
            own_ref[:, pl.ds(start, 256)], slab[:512, :], (((1,), (1,)), ((), ())), preferred_element_type=jnp.float32
        )
        total = part if total is None else total + part
    return total


def sums_kernel(count, order_ref, own_ref, *refs):
    total = products(order_ref, own_ref, refs[:count])
    refs[-1][...] = total + refs[count][...] if len(refs) > count + 1 else total


def sums(order, own, slabs, before=()):
    count = len(slabs)
    return pl.pallas_call(
        functools.partial(sums_kernel, count),
        in_specs=[smem(), vmem()] + [vmem()] * (count + len(before)),
        out_specs=vmem(),
        out_shape=jax.ShapeDtypeStruct((LAGS * 64, 512), jnp.float32),
        compiler_params=params(),
        cost_estimate=cost(2 * 960 * 512 * 256 * count, 2_000_000),
    )(order, own, *slabs, *before)


def place_round(out_ref, index, values, lags):
    for k in range(lags):
        rows = values[k * 64 : k * 64 + 64].astype(out_ref.dtype)
        out_ref[:, index, k * 512 : k * 512 + 512] = rows


def near_kernel(order_ref, weight_ref, own_ref, here_ref, there_ref, out_ref, sum_ref):
    slabs = [ref.at[k] for ref in (here_ref, there_ref) for k in range(4)]
    sum_ref[...] = products(order_ref, own_ref, slabs) * weight_ref[0]
    for index in range(2):
        @pl.when(order_ref[8] == index)
        def _():
            place_round(out_ref, index, sum_ref, LAGS)


def near_round(order, weights, own, here, there):
    return pl.pallas_call(
        near_kernel,
        in_specs=[smem(), smem()] + [vmem()] * 3,
        out_specs=vmem(),
        out_shape=jax.ShapeDtypeStruct((64, 2, LAGS * 512), jnp.bfloat16),
        scratch_shapes=[pltpu.VMEM((LAGS * 64, 512), jnp.float32)],
        compiler_params=params(),
        cost_estimate=cost(2 * 960 * 512 * 256 * 8, 4_000_000),
    )(order, weights, own, here, there)


def last_kernel(count, order_ref, weight_ref, own_ref, near_ref, part_ref, *refs):
    out_ref, sum_ref = refs[count], refs[count + 1]
    step = pl.program_id(0)

    @pl.when(step == 0)
    def _():
        sum_ref[...] = (products(order_ref, own_ref, refs[:count]) + part_ref[...]) * weight_ref[1]

    width = GROUP * 512
    out_ref[...] = near_ref[:, :, pl.ds(pl.multiple_of(step * width, width), width)]
    rows = sum_ref.at[pl.ds(pl.multiple_of(step * GROUP * 64, GROUP * 64), GROUP * 64)]
    for index in range(2):
        @pl.when(order_ref[count] != index)
        def _():
            place_round(out_ref, index, rows, GROUP)


def last_round(order, weights, own, near, part, slabs):
    count = len(slabs)
    return pl.pallas_call(
        functools.partial(last_kernel, count),
        grid=(LAGS // GROUP,),
        in_specs=[smem(), smem()] + [vmem()] * (3 + count),
        out_specs=pl.BlockSpec((64, 2, GROUP * 512), lambda g: (0, 0, g)),
        out_shape=jax.ShapeDtypeStruct((64, 2, LAGS * 512), jnp.bfloat16),
        scratch_shapes=[pltpu.VMEM((LAGS * 64, 512), jnp.float32)],
        compiler_params=params(),
        cost_estimate=cost(2 * 960 * 512 * 256 * count, 6_000_000),
    )(order, weights, own, near, part, *slabs)


def on_device(returns, plan, pair_mask):
    block = lax.axis_index("blk")
    z = lax.axis_index("tm_0")
    core = lax.axis_index("tm_1")
    minutes_all = returns.shape[1] * 8
    factor = float(minutes_all) ** (-0.5)

    words = (plan[0, 0], plan[1, 0])
    swap = (words[1] & 16) == 0
    near_word = jnp.where(swap, words[1], words[0])
    far_word = jnp.where(swap, words[0], words[1])
    near_live = pair_mask[block, block ^ near_word].astype(jnp.float32)
    far_live = pair_mask[block, block ^ far_word].astype(jnp.float32)
    weights = jnp.stack([near_live, far_live]) * factor

    def other_core(slabs):
        return [swapped(s, "tm_1", 1) for s in slabs]

    def order_of(words, extra=()):
        here = [2 * (z ^ k) + core for k in words]
        there = [2 * (z ^ k) + (1 - core) for k in words]
        return jnp.stack([jnp.int32(v) for v in here + there + list(extra)])

    far = by_word(returns, far_word & 15, 16, to_near)
    far_2, far_1 = crossed(far, 2), crossed(far, 1)
    near_word, _ = together(near_word, far)
    near = by_word(returns, near_word & 15, 16, to_near)
    near = lax.cond(near_word >= 16, lambda v: swapped(v, "blk", 16), lambda v: v, near)
    rows = returns.reshape(4, 128, returns.shape[1])
    packs = []
    for k in range(4):
        pack = jnp.concatenate([near, lax.dynamic_index_in_dim(rows, z ^ k, 0, keepdims=False)], axis=0)
        packs.append(swapped(pack, "tm_0", k) if k else pack)
    far_2, far_1, weights = together(far_2, far_1, weights)
    far_3, far_0 = swapped(far_2, "tm_0", 1), swapped(far_1, "tm_0", 1)
    packs = list(together(*packs, far_3, far_1)[:4])
    near_here = jnp.stack(packs)
    near_there = swapped(near_here, "tm_1", 1)
    own = own_shifts(jnp.stack([z, core]).astype(jnp.int32), near_here, near_there)
    near_index = swap.astype(jnp.int32)
    done = near_round(order_of(range(4), [near_index]), weights, own, near_here, near_there)
    part = sums(order_of([2, 1]), own, [far_2, far_1] + other_core([far_2, far_1]))
    far_3, far_0, done, part = together(far_3, far_0, done, part)
    order = order_of([3, 0])
    part = sums(order[:2], own, [far_3, far_0], (part,))
    order = jnp.concatenate([order[2:], near_index.reshape(1)])
    return last_round(order, weights, own, done, part, other_core([far_3, far_0]))


def solution(mesh):
    split = Mesh(mesh.devices.reshape(mesh.shape["blk"], 4, 2), ("blk", "tm_0", "tm_1"))
    return jax.shard_map(
        on_device,
        mesh=split,
        in_specs=(P("blk", TM), P(), P()),
        out_specs=P(BLK_TM, None, None),
        check_vma=False,
    )
```

```python
import functools

import jax
import jax.numpy as jnp
from jax import lax
from jax.experimental import pallas as pl
from jax.experimental.pallas import tpu as pltpu
from jax.sharding import Mesh
from jax.sharding import PartitionSpec as P

LAG = 7
LAGS = 2 * LAG + 1
TM = ("tm_0", "tm_1")
BLK_TM = ("blk", "tm_0", "tm_1")
GROUP = 15
VMEM_BYTES = 20 * 1024 * 1024

def swapped(value, axis, word):
    count = lax.axis_size(axis)
    return lax.ppermute(value, axis, [(i, i ^ word) for i in range(count)])


def crossed(value, word):
    count = lax.axis_size("blk") * 4
    return lax.ppermute(value, ("blk", "tm_0"), [(i, i ^ 64 ^ word) for i in range(count)])


def together(*values):
    return lax.optimization_barrier(values)


def by_word(value, word, count, move):
    return lax.switch(word, [functools.partial(move, word=k) for k in range(count)], value)


def to_near(value, word):
    return swapped(value, "blk", word) if word else value


def vmem():
    return pl.BlockSpec(memory_space=pltpu.VMEM)


def smem():
    return pl.BlockSpec(memory_space=pltpu.SMEM)


def params():
    return pltpu.CompilerParams(vmem_limit_bytes=VMEM_BYTES)


def cost(flops, size):
    return pl.CostEstimate(flops=flops, bytes_accessed=size, transcendentals=0)


def own_kernel(place_ref, here_ref, there_ref, out_ref, row_ref):
    z, core = place_ref[0], place_ref[1]
    rows, edge = row_ref.shape[0], 128
    row_ref[:, :edge] = jnp.zeros((rows, edge), row_ref.dtype)
    row_ref[:, edge + 2048 :] = jnp.zeros((rows, edge), row_ref.dtype)
    mine = pl.ds(pl.multiple_of(512 + core * rows, 64), rows)
    for k in range(4):
        slab = 2 * (z ^ k)
        for pack, at in ((here_ref, slab + core), (there_ref, slab + 1 - core)):
            row_ref[:, pl.ds(pl.multiple_of(edge + at * 256, 128), 256)] = pack[k, mine, :]
    for lag in range(LAGS):
        start = edge + LAG - lag
        out_ref[lag * rows : lag * rows + rows, :] = row_ref[:, start : start + 2048]


def own_shifts(place, here, there):
    return pl.pallas_call(
        own_kernel,
        in_specs=[smem()] + [vmem()] * 2,
        out_specs=vmem(),
        out_shape=jax.ShapeDtypeStruct((LAGS * 64, 2048), jnp.bfloat16),
        scratch_shapes=[pltpu.VMEM((64, 2048 + 256), jnp.bfloat16)],
        compiler_params=params(),
        cost_estimate=cost(0, 8_000_000),
    )(place, here, there)


def products(order_ref, own_ref, slab_refs):
    total = None
    for k, slab in enumerate(slab_refs):
        start = pl.multiple_of(order_ref[k] * 256, 256)
        part = lax.dot_general(
            own_ref[:, pl.ds(start, 256)], slab[:512, :], (((1,), (1,)), ((), ())), preferred_element_type=jnp.float32
        )
        total = part if total is None else total + part
    return total


def sums_kernel(count, order_ref, own_ref, *refs):
    total = products(order_ref, own_ref, refs[:count])
    refs[-1][...] = total + refs[count][...] if len(refs) > count + 1 else total


def sums(order, own, slabs, before=()):
    count = len(slabs)
    return pl.pallas_call(
        functools.partial(sums_kernel, count),
        in_specs=[smem(), vmem()] + [vmem()] * (count + len(before)),
        out_specs=vmem(),
        out_shape=jax.ShapeDtypeStruct((LAGS * 64, 512), jnp.float32),
        compiler_params=params(),
        cost_estimate=cost(2 * 960 * 512 * 256 * count, 2_000_000),
    )(order, own, *slabs, *before)


def place_round(out_ref, index, values, lags):
    for k in range(lags):
        rows = values[k * 64 : k * 64 + 64].astype(out_ref.dtype)
        out_ref[:, index, k * 512 : k * 512 + 512] = rows


def near_kernel(order_ref, weight_ref, own_ref, here_ref, there_ref, out_ref, sum_ref):
    slabs = [ref.at[k] for ref in (here_ref, there_ref) for k in range(4)]
    sum_ref[...] = products(order_ref, own_ref, slabs) * weight_ref[0]
    for index in range(2):
        @pl.when(order_ref[8] == index)
        def _():
            place_round(out_ref, index, sum_ref, LAGS)


def near_round(order, weights, own, here, there):
    return pl.pallas_call(
        near_kernel,
        in_specs=[smem(), smem()] + [vmem()] * 3,
        out_specs=vmem(),
        out_shape=jax.ShapeDtypeStruct((64, 2, LAGS * 512), jnp.bfloat16),
        scratch_shapes=[pltpu.VMEM((LAGS * 64, 512), jnp.float32)],
        compiler_params=params(),
        cost_estimate=cost(2 * 960 * 512 * 256 * 8, 4_000_000),
    )(order, weights, own, here, there)


def last_kernel(count, order_ref, weight_ref, own_ref, near_ref, part_ref, *refs):
    out_ref, sum_ref = refs[count], refs[count + 1]
    step = pl.program_id(0)

    @pl.when(step == 0)
    def _():
        sum_ref[...] = (products(order_ref, own_ref, refs[:count]) + part_ref[...]) * weight_ref[1]

    width = GROUP * 512
    out_ref[...] = near_ref[:, :, pl.ds(pl.multiple_of(step * width, width), width)]
    rows = sum_ref.at[pl.ds(pl.multiple_of(step * GROUP * 64, GROUP * 64), GROUP * 64)]
    for index in range(2):
        @pl.when(order_ref[count] != index)
        def _():
            place_round(out_ref, index, rows, GROUP)


def last_round(order, weights, own, near, part, slabs):
    count = len(slabs)
    return pl.pallas_call(
        functools.partial(last_kernel, count),
        grid=(LAGS // GROUP,),
        in_specs=[smem(), smem()] + [vmem()] * (3 + count),
        out_specs=pl.BlockSpec((64, 2, GROUP * 512), lambda g: (0, 0, g)),
        out_shape=jax.ShapeDtypeStruct((64, 2, LAGS * 512), jnp.bfloat16),
        scratch_shapes=[pltpu.VMEM((LAGS * 64, 512), jnp.float32)],
        compiler_params=params(),
        cost_estimate=cost(2 * 960 * 512 * 256 * count, 6_000_000),
    )(order, weights, own, near, part, *slabs)


def on_device(returns, plan, pair_mask):
    block = lax.axis_index("blk")
    z = lax.axis_index("tm_0")
    core = lax.axis_index("tm_1")
    minutes_all = returns.shape[1] * 8
    factor = float(minutes_all) ** (-0.5)

    words = (plan[0, 0], plan[1, 0])
    swap = (words[1] & 16) == 0
    near_word = jnp.where(swap, words[1], words[0])
    far_word = jnp.where(swap, words[0], words[1])
    near_live = pair_mask[block, block ^ near_word].astype(jnp.float32)
    far_live = pair_mask[block, block ^ far_word].astype(jnp.float32)
    weights = jnp.stack([near_live, far_live]) * factor

    def other_core(slabs):
        return [swapped(s, "tm_1", 1) for s in slabs]

    def order_of(words, extra=()):
        here = [2 * (z ^ k) + core for k in words]
        there = [2 * (z ^ k) + (1 - core) for k in words]
        return jnp.stack([jnp.int32(v) for v in here + there + list(extra)])

    far = by_word(returns, far_word & 15, 16, to_near)
    far_2, far_1 = crossed(far, 2), crossed(far, 1)
    near_word, _ = together(near_word, far)
    near = by_word(returns, near_word & 15, 16, to_near)
    near = lax.cond(near_word >= 16, lambda v: swapped(v, "blk", 16), lambda v: v, near)
    rows = returns.reshape(4, 128, returns.shape[1])
    packs = []
    for k in range(4):
        pack = jnp.concatenate([near, lax.dynamic_index_in_dim(rows, z ^ k, 0, keepdims=False)], axis=0)
        packs.append(swapped(pack, "tm_0", k) if k else pack)
    far_2, far_1, weights = together(far_2, far_1, weights)
    far_3, far_0 = swapped(far_2, "tm_0", 1), swapped(far_1, "tm_0", 1)
    packs = list(together(*packs, far_3, far_1)[:4])
    near_here = jnp.stack(packs)
    near_there = swapped(near_here, "tm_1", 1)
    own = own_shifts(jnp.stack([z, core]).astype(jnp.int32), near_here, near_there)
    near_index = swap.astype(jnp.int32)
    done = near_round(order_of(range(4), [near_index]), weights, own, near_here, near_there)
    part = sums(order_of([2, 1]), own, [far_2, far_1] + other_core([far_2, far_1]))
    far_3, far_0, done, part = together(far_3, far_0, done, part)
    order = order_of([3, 0])
    part = sums(order[:2], own, [far_3, far_0], (part,))
    order = jnp.concatenate([order[2:], near_index.reshape(1)])
    return last_round(order, weights, own, done, part, other_core([far_3, far_0]))


def solution(mesh):
    split = Mesh(mesh.devices.reshape(mesh.shape["blk"], 4, 2), ("blk", "tm_0", "tm_1"))
    return jax.shard_map(
        on_device,
        mesh=split,
        in_specs=(P("blk", TM), P(), P()),
        out_specs=P(BLK_TM, None, None),
        check_vma=False,
    )
```
